32 devices in a mesh: chan: 8 (over y, x, core), pulse: 4 (over z).
Axes of the slice: x: 2, y: 2, z: 4, core: 2. Of those that a mesh axis runs over, the one named last changes fastest.
Arguments:
- echoes: float32 [8, 2, 4096, 4096], P('chan', None, 'pulse'), may hold values from -6 to 6
- chirp_phase: float32 [4096], replicated, may hold values from -3.140625 to 3.140625
- rcmc_kernel: float32 [32, 128, 128], P('pulse'), may hold values from -0.5 to 0.5
- rcmc_offset: int32 [32], P('pulse'), may hold values from 1 to 64, as said below
- az_phase: float32 [4096, 32], P(None, 'pulse'), may hold values from -3.140625 to 3.140625
- weight_table: float32 [2, 64], replicated, may hold values from -1.5 to 1.5
- weight_index: int32 [8, 32], P('chan'), may hold values from 0 to 63
Outputs:
- image: float32 [2, 4096, 4096], P(None, 'chan', 'pulse')
The draws below stay inside these ranges and needn't reach their ends.
Inputs may be any that keep to these rules, and one draw needn't show every extreme that they name: `rcmc_offset`: every offset is at least 1, and in every draw some block's offset equals 64.
All inputs are finite; a program needn't handle non-finite values.
Results may differ from the reference program's by a relative error of at most 0.0001.
Values sent between devices are 32-bit elements; how exact they have to be, the bound alone decides.
A program may use at most 256 MiB of HBM per device.

```python
import jax
import jax.numpy as jnp
from jax import lax

PULSES = 4096
GATES = 4096
BLOCK = 128
DBLOCK = 128
TABLE = 64
CHAN = 8
HALF = 64
NBLK = 32
NDBLK = 32


def draw_rcmc_offset(key, part):
    first_key, second_key = jax.random.split(jax.random.fold_in(key, 17))
    offsets_drawn = jax.random.randint(first_key, (NBLK,), 1, HALF + 1)
    forced_spot = jax.random.randint(second_key, (), 0, NBLK)
    return jnp.where(jnp.arange(NBLK) == forced_spot, HALF, offsets_drawn).astype(jnp.int32)


def set_ends(drawn, own_key, least, high):
    index_at = [jax.random.randint(jax.random.fold_in(own_key, axis), (), 0, length) for axis, length in enumerate(drawn.shape)]
    main_axis = drawn.shape.index(max(drawn.shape))
    neighbour = index_at[:main_axis] + [(index_at[main_axis] + 1) % drawn.shape[main_axis]] + index_at[main_axis + 1:]
    return drawn.at[tuple(index_at)].set(least).at[tuple(neighbour)].set(high)


def level_of(key, shape, shards, smallest, high):
    loudness = 1.0
    for axis_at, parts in shards:
        heights = jax.random.uniform(jax.random.fold_in(jax.random.fold_in(key, 6), axis_at), (parts,), jnp.float32, smallest / len(shards), high / len(shards))
        loudness = loudness * jnp.repeat(jnp.exp(heights), shape[axis_at] // parts).reshape((-1,) + (1,) * (len(shape) - 1 - axis_at))
    return loudness


def gaussian(rng, shape, scale, limit, cuts=(), held_as=jnp.bfloat16):
    gain = level_of(rng, shape, cuts, -0.22, 0.18) if cuts else 1.0
    array = jax.random.normal(rng, shape, jnp.float32) * scale * gain
    return jnp.minimum(jnp.maximum(array, -limit), limit).astype(held_as)


def setup_inputs(seed: int = 0) -> dict:
    keys = jax.random.split(jax.random.key(seed), 8)
    return {
        "echoes": gaussian(keys[0], (CHAN, 2, PULSES, GATES), 1.0, 6.0, ((0, 8), (2, 4)), jnp.float32),
        "chirp_phase": jnp.clip(jax.random.uniform(keys[1], (GATES,), jnp.float32, -3.140625, 3.140625), -3.140625, 3.140625),
        "rcmc_kernel": gaussian(keys[2], (NBLK, BLOCK, BLOCK), BLOCK ** -0.5, 0.5, ((0, 4),), jnp.float32),
        "rcmc_offset": draw_rcmc_offset(jax.random.fold_in(keys[7], 71), 0),
        "az_phase": jnp.clip(jax.random.uniform(keys[4], (PULSES, NBLK), jnp.float32, -3.140625, 3.140625), -3.140625, 3.140625),
        "weight_table": gaussian(keys[5], (2, TABLE), 0.25, 1.5, (), jnp.float32),
        "weight_index": set_ends(jax.random.randint(keys[6], (CHAN, NDBLK), 0, TABLE), jax.random.fold_in(keys[6], 1), 0, TABLE - 1).astype(jnp.int32),
    }


def channel_image(channel_echo, index_row, chirp_phase, rcmc_kernel, rcmc_offset, az_phase, weight_table):
    signal = lax.complex(channel_echo[0], channel_echo[1])
    spectrum = jnp.fft.fft(signal, axis=1, norm="ortho")
    chirp = lax.complex(jnp.cos(chirp_phase), jnp.sin(chirp_phase))
    compressed = jnp.fft.ifft(spectrum * chirp[None, :], axis=1, norm="ortho")
    doppler = jnp.fft.fft(compressed, axis=0, norm="ortho")
    padded = jnp.pad(doppler, ((0, 0), (0, HALF)))
    starts = jnp.arange(NBLK, dtype=jnp.int32) * BLOCK + rcmc_offset.astype(jnp.int32)
    gather_index = (starts[:, None] + jnp.arange(BLOCK, dtype=jnp.int32)[None, :]).reshape(-1)
    windows = jnp.take(padded, gather_index, axis=1).reshape(PULSES, NBLK, BLOCK)
    mig_re = jnp.einsum("pbj,bji->pbi", jnp.real(windows), rcmc_kernel, precision=lax.Precision.HIGHEST)
    mig_im = jnp.einsum("pbj,bji->pbi", jnp.imag(windows), rcmc_kernel, precision=lax.Precision.HIGHEST)
    migrated = lax.complex(mig_re, mig_im).reshape(PULSES, GATES)
    phase_factor = jnp.repeat(lax.complex(jnp.cos(az_phase), jnp.sin(az_phase)), BLOCK, axis=1)
    weights = lax.complex(weight_table[0, index_row], weight_table[1, index_row])
    weight_full = jnp.repeat(weights, DBLOCK)[:, None]
    filtered = migrated * phase_factor * weight_full
    focused = jnp.fft.ifft(filtered, axis=0, norm="ortho")
    return jnp.stack([jnp.real(focused), jnp.imag(focused)])


def reference(echoes, chirp_phase, rcmc_kernel, rcmc_offset, az_phase, weight_table, weight_index):
    def add_channel(running, scan_item):
        channel_echo, index_row = scan_item
        term = channel_image(channel_echo, index_row, chirp_phase, rcmc_kernel, rcmc_offset, az_phase, weight_table)
        return running + term, None

    start_value = jnp.zeros((2, PULSES, GATES), jnp.float32)
    running, _ = lax.scan(add_channel, start_value, (echoes, weight_index))
    return running
```

```python
import math

import jax
import jax.numpy as jnp
from jax import lax
from jax.sharding import PartitionSpec as P

BLOCK = 128
CHUNKS = 4
PRECISION = lax.Precision.HIGH


def factor_pair(length):
    return (128, length // 128)


def unit_table(count_a, count_b, modulus, sign_value, start_a=0):
    row_index = lax.broadcasted_iota(jnp.int32, (count_a, count_b), 0) + start_a
    col_index = lax.broadcasted_iota(jnp.int32, (count_a, count_b), 1)
    angles = (
        sign_value * 2.0 * math.pi / modulus * (row_index * col_index % modulus).astype(jnp.float32)
    )
    return (jnp.cos(angles), jnp.sin(angles))


def realify(coef_re, coef_im):
    return jnp.stack([jnp.stack([coef_re, coef_im]), jnp.stack([-coef_im, coef_re])])


def transform(stacked, sign_value, along_rows, prefactor=None):
    length = stacked.shape[1] if along_rows else stacked.shape[2]
    inner_len, outer_len = factor_pair(length)
    outer_re, outer_im = unit_table(outer_len, outer_len, outer_len, sign_value)
    inner_re, inner_im = unit_table(inner_len, inner_len, inner_len, sign_value)
    twist_re, twist_im = unit_table(outer_len, inner_len, length, sign_value)
    first_re = (
        outer_re[:, :, None] * twist_re[None, :, :] - outer_im[:, :, None] * twist_im[None, :, :]
    )
    first_im = (
        outer_re[:, :, None] * twist_im[None, :, :] + outer_im[:, :, None] * twist_re[None, :, :]
    )
    if prefactor is not None:
        pre_re = jnp.cos(prefactor).reshape(outer_len, inner_len)[:, None, :]
        pre_im = jnp.sin(prefactor).reshape(outer_len, inner_len)[:, None, :]
        first_re, first_im = (
            first_re * pre_re - first_im * pre_im,
            first_re * pre_im + first_im * pre_re,
        )
    first_table = realify(first_re, first_im)
    norm_scale = 1.0 / math.sqrt(length)
    second_table = realify(inner_re * norm_scale, inner_im * norm_scale)
    if along_rows:
        col_count = stacked.shape[2]
        data = stacked.reshape(2, outer_len, inner_len, col_count)
        middle = jnp.einsum("sabc,stakb->tkbc", data, first_table, precision=PRECISION)
        result = jnp.einsum("tkbc,tubj->ujkc", middle, second_table, precision=PRECISION)
        return result.reshape(2, length, col_count)
    row_count = stacked.shape[1]
    data = stacked.reshape(2, row_count, outer_len, inner_len)
    middle = jnp.einsum("srab,stakb->trkb", data, first_table, precision=PRECISION)
    result = jnp.einsum("trkb,tubj->urjk", middle, second_table, precision=PRECISION)
    return result.reshape(2, row_count, length)


def body(echoes, chirp_phase, rcmc_kernel, rcmc_offset, az_phase, weight_table, weight_index):
    own = echoes[0]
    pulses_dev, gates = own.shape[1], own.shape[2]
    chans = lax.axis_size("chan")
    pulse_devs = lax.axis_size("pulse")
    pulses = pulses_dev * pulse_devs
    dblocks = weight_index.shape[1]
    bins = pulses // dblocks
    coarse = pulses_dev // dblocks
    z = lax.axis_index("pulse")
    j = lax.axis_index("chan")

    kernels = lax.all_gather(rcmc_kernel, "pulse", axis=0, tiled=True)
    offsets = lax.all_gather(rcmc_offset, "pulse", axis=0, tiled=True)
    phases = lax.all_gather(az_phase, "pulse", axis=1, tiled=True)
    indices = lax.all_gather(weight_index[0], "chan", axis=0, tiled=False)

    fine_re, fine_im = unit_table(pulses_dev, bins, pulses, -1.0, z * pulses_dev)
    fine = realify(fine_re, fine_im).reshape(2, 2, coarse, dblocks, bins)
    entry_ids = lax.broadcasted_iota(jnp.int32, (chans, dblocks, weight_table.shape[1]), 2)
    one_hot = (indices[:, :, None] == entry_ids).astype(jnp.float32)
    chosen = jnp.einsum("cen,wn->wce", one_hot, weight_table, precision=lax.Precision.HIGHEST)
    step_re, step_im = unit_table(dblocks, dblocks, dblocks, -1.0)
    norm_scale = 1.0 / math.sqrt(pulses)
    w_re, w_im = chosen[0][:, None, :] * norm_scale, chosen[1][:, None, :] * norm_scale
    mix = realify(step_re * w_re - step_im * w_im, step_re * w_im + step_im * w_re)

    width = gates // CHUNKS
    parts = []
    for chunk in range(CHUNKS):
        piece = own[:, :, chunk * width : (chunk + 1) * width]
        piece = piece.reshape(2, pulses_dev, chans, width // chans)
        piece = jnp.transpose(piece, (2, 0, 1, 3))
        held = lax.all_to_all(piece, "chan", split_axis=0, concat_axis=0, tiled=True)
        held = held.reshape(chans, 2, coarse, dblocks, width // chans)
        middle = jnp.einsum("csabg,stabr->bctrg", held, fine, precision=PRECISION)
        summed = jnp.einsum("bctrg,tucbe->uerg", middle, mix, precision=PRECISION)
        summed = summed.reshape(2, pulses, width // chans)
        parts.append(lax.psum_scatter(summed, "pulse", scatter_dimension=1, tiled=True))

    joined = jnp.stack(parts)
    rows = joined.shape[2] // chans
    joined = joined.reshape(CHUNKS, 2, chans, rows, width // chans)
    joined = jnp.transpose(joined, (2, 0, 1, 3, 4))
    joined = lax.all_to_all(joined, "chan", split_axis=0, concat_axis=0, tiled=True)
    doppler = jnp.transpose(joined, (2, 3, 1, 0, 4)).reshape(2, rows, gates)

    spectrum = transform(doppler, -1.0, False)
    compressed = transform(spectrum, 1.0, False, chirp_phase)
    blocks = gates // BLOCK
    split = compressed.reshape(2, rows, blocks, BLOCK)
    after = jnp.pad(split[:, :, 1:], ((0, 0), (0, 0), (0, 1), (0, 0)))
    window = jnp.concatenate([split, after], axis=3)
    at = lax.broadcasted_iota(jnp.int32, (blocks, 2 * BLOCK, BLOCK), 1)
    lane = lax.broadcasted_iota(jnp.int32, (blocks, 2 * BLOCK, BLOCK), 2)
    selector = (at == offsets[:, None, None] + lane).astype(jnp.float32)
    banded = jnp.einsum("brj,bjm->brm", selector, kernels, precision=lax.Precision.HIGHEST)
    migrated = jnp.einsum("sdbr,brm->sdbm", window, banded, precision=PRECISION)

    angle = lax.dynamic_slice_in_dim(phases, (z * chans + j) * rows, rows, axis=0)
    cos, sin = jnp.cos(angle)[:, :, None], jnp.sin(angle)[:, :, None]
    filtered = jnp.stack(
        [migrated[0] * cos - migrated[1] * sin, migrated[0] * sin + migrated[1] * cos]
    ).reshape(2, rows, gates)

    shares = lax.all_to_all(filtered, ("pulse", "chan"), split_axis=2, concat_axis=1, tiled=True)
    focused = transform(shares, 1.0, True)
    return lax.all_to_all(focused, "chan", split_axis=1, concat_axis=2, tiled=True)


def solution(mesh):
    return jax.shard_map(
        body,
        mesh=mesh,
        in_specs=(
            P("chan", None, "pulse", None),
            P(),
            P("pulse", None, None),
            P("pulse"),
            P(None, "pulse"),
            P(),
            P("chan", None),
        ),
        out_specs=P(None, "chan", "pulse"),
        check_vma=False,
    )
```
